32 devices in a mesh: dp: 4 (over y, x), tensor: 8 (over z, core).
Axes of the slice: x: 2, y: 2, z: 4, core: 2. Of those that a mesh axis runs over, the one named last changes fastest.
Arguments:
- grad_out: bfloat16 [2048, 8192], P('dp', 'tensor'), may hold values from -6 to 6
- down_weight: bfloat16 [8192, 24576], P(None, 'tensor'), may hold values from -0.0625 to 0.0625
- quantized: bfloat16 [2048, 24576], P('dp', 'tensor'), may hold values from -0.125 to 0.125
- clip_mask: int32 [2048, 24576], P('dp', 'tensor'), may hold values 0 or 1
- first_rot: bfloat16 [192, 128, 128], P('tensor'), may hold values from -0.5 to 0.5
- second_rot: bfloat16 [192, 128, 128], P('tensor'), may hold values from -0.5 to 0.5
- block_order: int32 [192], replicated, may hold values from 0 to 191, each once
Outputs:
- grad_hidden: bfloat16 [2048, 24576], P('dp', 'tensor')
- grad_weight: bfloat16 [8192, 24576], P('dp', 'tensor')
The draws below stay inside these ranges and needn't reach their ends.
Inputs may be any that keep to these rules, and one draw needn't show every extreme that they name: `block_order`: a permutation of the blocks.
All inputs are finite; a program needn't handle non-finite values. No bound on the sum of `clip_mask` on one device may be relied on, other than what follows from the above.
Results may differ from the reference program's by a relative error of at most 0.009.
Values may be sent and summed in bfloat16 or wider, within the bound.
No kernel may reach another device: no remote copies, remote signals or barrier semaphores. Data moves between devices by JAX's collectives and lax.ppermute only.
A program may use at most 320 MiB of HBM per device.

```python
import jax
import jax.numpy as jnp
from jax import lax

D = 8192
FF = 24576
BS = 128
TOK_DEV = 512
BLOCKS = 192
TOKENS = 2048
N_DP = 4


def place_ends(values, key, low, high):
    place = [jax.random.randint(jax.random.fold_in(key, axis), (), 0, length) for axis, length in enumerate(values.shape)]
    longest = values.shape.index(max(values.shape))
    next_to = place[:longest] + [(place[longest] + 1) % values.shape[longest]] + place[longest + 1:]
    return values.at[tuple(place)].set(low).at[tuple(next_to)].set(high)


def levels(stream_key, dims, cuts, smallest, largest):
    level = 1.0
    for dim, blocks in cuts:
        heights = jax.random.uniform(jax.random.fold_in(jax.random.fold_in(stream_key, 6), dim), (blocks,), jnp.float32, smallest / len(cuts), largest / len(cuts))
        level = level * jnp.repeat(jnp.exp(heights), dims[dim] // blocks).reshape((-1,) + (1,) * (len(dims) - 1 - dim))
    return level


def normal_values(key, shape, width, bound, cuts=(), kind=jnp.bfloat16):
    values = width * jax.random.normal(key, shape, jnp.float32)
    if cuts:
        values = values * levels(key, shape, cuts, -0.22, 0.18)
    return jnp.clip(values, -bound, bound).astype(kind)


def setup_inputs(seed: int = 0) -> dict:
    splits = jax.random.split(jax.random.key(seed), 8)
    return {
        "grad_out": normal_values(splits[0], (TOKENS, D), 1.0, 6.0, ((0, 4), (1, 8))),
        "down_weight": normal_values(splits[1], (D, FF), D ** -0.5, 0.0625, ((1, 8),)),
        "quantized": normal_values(splits[2], (TOKENS, FF), TOKENS ** -0.5, 0.125, ((0, 4), (1, 8))),
        "clip_mask": place_ends((jax.random.randint(splits[3], (TOKENS, FF), 0, 10) < 9).astype(jnp.int32), jax.random.fold_in(splits[3], 1), 0, 1),
        "first_rot": normal_values(splits[4], (BLOCKS, BS, BS), BS ** -0.5, 0.5, ((0, 8),)),
        "second_rot": normal_values(splits[5], (BLOCKS, BS, BS), BS ** -0.5, 0.5, ((0, 8),)),
        "block_order": jax.random.permutation(splits[6], BLOCKS).astype(jnp.int32),
    }


def block_apply(values, rotations):
    shaped = values.reshape(values.shape[0], BLOCKS, BS).astype(jnp.float32)
    result = jnp.einsum("tbi,bji->tbj", shaped, rotations.astype(jnp.float32))
    return result.reshape(values.shape[0], FF).astype(jnp.bfloat16)


def reference(grad_out, down_weight, quantized, clip_mask, first_rot, second_rot, block_order):
    product = jnp.dot(grad_out, down_weight, preferred_element_type=jnp.float32)
    masked = (product * clip_mask).astype(jnp.bfloat16)
    permuted = block_apply(masked, second_rot)
    inverse = jnp.zeros((BLOCKS,), jnp.int32).at[block_order].set(jnp.arange(BLOCKS, dtype=jnp.int32))
    blocked = permuted.reshape(TOKENS, BLOCKS, BS)
    unpermuted = jnp.take(blocked, inverse, axis=1).reshape(TOKENS, FF)
    grad_hidden = block_apply(unpermuted, first_rot)
    groups_out = grad_out.reshape(N_DP, TOK_DEV, D)
    groups_act = quantized.reshape(N_DP, TOK_DEV, FF)

    def add_group(total, pair):
        partial_value = lax.dot_general(pair[0], pair[1], (((0,), (0,)), ((), ())), preferred_element_type=jnp.float32)
        return total + partial_value.astype(jnp.bfloat16).astype(jnp.float32), None

    total, unused = lax.scan(add_group, jnp.zeros((D, FF), jnp.float32), (groups_out, groups_act))
    return grad_hidden, total.astype(jnp.bfloat16)
```

```python
import functools

import jax
import jax.numpy as jnp
from jax import lax
from jax.experimental import pallas as pl
from jax.experimental.pallas import tpu as pltpu
from jax.sharding import PartitionSpec as P

CHUNKS = 2
VMEM_LIMIT = 56 * 1024 * 1024
ANY = pl.BlockSpec(memory_space=pl.ANY)


def rows_at(index, count):
    return pl.ds(pl.multiple_of(index * count, count), count)


def params(limit=VMEM_LIMIT):
    return pltpu.CompilerParams(vmem_limit_bytes=limit)


def cost(flops, nbytes):
    return pl.CostEstimate(flops=int(flops), bytes_accessed=int(nbytes), transcendentals=0)


def project_kernel(devices, groups, tile, chunk, place_ref, *refs):
    given = len(refs) - groups - 7
    bufs, (w_ref, mask_ref, rot_ref, out_ref) = refs[:given], refs[given : given + 4]
    shards, (dy, sems, shard_sems) = refs[given + 4 : -3], refs[-3:]
    me, group = place_ref[0], place_ref[1]
    rows, width = dy.shape[0], dy.shape[1] // devices

    def gather(action):
        for x in range(devices):
            if len(bufs) == 1:
                source, shard = bufs[0].at[x], x
            else:
                source, shard = bufs[x], me ^ x
            if source.shape[0] != rows:
                source = source.at[chunk * rows : (chunk + 1) * rows]
            action(pltpu.make_async_copy(source, dy.at[:, rows_at(shard, width)], sems.at[x]))

    def share(action):
        for m, shard in enumerate(shards):
            source = dy.at[:, rows_at(2 * (group ^ m) + me % 2, width)]
            action(pltpu.make_async_copy(source, shard, shard_sems.at[m]))

    @pl.when(pl.program_id(0) == 0)
    def _():
        gather(lambda copy: copy.start())
        gather(lambda copy: copy.wait())
        share(lambda copy: copy.start())

    product = jnp.dot(dy[...], w_ref[...], preferred_element_type=jnp.float32)
    masked = (product * mask_ref[...].astype(jnp.float32)).astype(jnp.bfloat16)
    block = rot_ref.shape[1]
    for b in range(tile // block):
        turned = lax.dot_general(
            masked[:, b * block : (b + 1) * block],
            rot_ref[b],
            (((1,), (1,)), ((), ())),
            preferred_element_type=jnp.float32,
        )
        out_ref[:, b * block : (b + 1) * block] = turned.astype(jnp.bfloat16)

    @pl.when(pl.program_id(0) == pl.num_programs(0) - 1)
    def _():
        share(lambda copy: copy.wait())


def project(place, bufs, weight, mask, rot, chunk, groups, tile_blocks=4):
    rows, width = bufs[-1].shape[-2:]
    depth, units = weight.shape
    devices = depth // width
    block = rot.shape[1]
    tile = tile_blocks * block
    permuted, *shards = pl.pallas_call(
        functools.partial(project_kernel, devices, groups, tile, chunk),
        grid_spec=pltpu.PrefetchScalarGridSpec(
            num_scalar_prefetch=1,
            grid=(units // tile,),
            in_specs=[ANY] * len(bufs)
            + [
                pl.BlockSpec((depth, tile), lambda j, _: (0, j)),
                pl.BlockSpec((rows, tile), lambda j, _: (chunk, j)),
                pl.BlockSpec((tile // block, block, block), lambda j, _: (j, 0, 0)),
            ],
            out_specs=[pl.BlockSpec((rows, tile), lambda j, _: (0, j))] + [ANY] * groups,
            scratch_shapes=[
                pltpu.VMEM((rows, depth), jnp.bfloat16),
                pltpu.SemaphoreType.DMA((devices,)),
                pltpu.SemaphoreType.DMA((groups,)),
            ],
        ),
        out_shape=[jax.ShapeDtypeStruct((rows, units), jnp.bfloat16)]
        + [jax.ShapeDtypeStruct((rows, width), jnp.bfloat16)] * groups,
        compiler_params=params(),
        cost_estimate=cost(2 * rows * depth * units, 2 * depth * units + 2 * rows * depth + 8 * rows * units),
    )(place, *bufs, weight, mask, rot)
    return permuted, shards


def reorder_kernel(block, order_ref, in_ref, out_ref):
    per = in_ref.shape[2] // block
    for source in range(in_ref.shape[0]):
        for b in range(per):
            to = order_ref[source * per + b]
            out_ref[to // per, :, rows_at(to % per, block)] = in_ref[source, :, b * block : (b + 1) * block]


def reorder(order, pieces, block):
    devices, rows, units = pieces.shape
    step = min(rows, 16)
    spec = pl.BlockSpec((devices, step, units), lambda i, _: (0, i, 0))
    return pl.pallas_call(
        functools.partial(reorder_kernel, block),
        grid_spec=pltpu.PrefetchScalarGridSpec(
            num_scalar_prefetch=1, grid=(rows // step,), in_specs=[spec], out_specs=spec
        ),
        out_shape=jax.ShapeDtypeStruct(pieces.shape, jnp.bfloat16),
        compiler_params=params(),
        cost_estimate=cost(0, 4 * devices * rows * units),
    )(order, pieces)


def rotate_kernel(piece_ref, rot_ref, *refs):
    out_ref = refs[-1]
    block = rot_ref.shape[1]
    for b in range(rot_ref.shape[0]):
        turned = lax.dot_general(
            piece_ref[:, b * block : (b + 1) * block],
            rot_ref[b],
            (((1,), (1,)), ((), ())),
            preferred_element_type=jnp.float32,
        )
        out_ref[:, b * block : (b + 1) * block] = turned.astype(jnp.bfloat16)


def rotate(piece, rot, chunk, chunks, so_far):
    rows, units = piece.shape
    block = rot.shape[1]
    tile = 8 * block
    held = [] if so_far is None else [so_far]
    return pl.pallas_call(
        rotate_kernel,
        grid=(units // tile,),
        in_specs=[
            pl.BlockSpec((rows, tile), lambda j: (0, j)),
            pl.BlockSpec((tile // block, block, block), lambda j: (j, 0, 0)),
        ]
        + [ANY] * len(held),
        out_specs=pl.BlockSpec((rows, tile), lambda j: (chunk, j)),
        out_shape=jax.ShapeDtypeStruct((rows * chunks, units), jnp.bfloat16),
        input_output_aliases={2: 0} if held else {},
        compiler_params=params(),
        cost_estimate=cost(2 * rows * units * block, 4 * rows * units),
    )(piece, rot, *held)


def weight_kernel(count, place_ref, *refs):
    pieces, values, (out_ref, turned) = refs[:count], refs[count:-2], refs[-2:]
    rows = pieces[0].shape[0]

    @pl.when(pl.program_id(0) == 0)
    def _():
        for n, piece in enumerate(pieces):
            turned[:, n * rows : (n + 1) * rows] = piece[...].T

    total, at = None, 0
    for value in values:
        tokens = value.shape[0]
        part = jnp.dot(turned[:, at : at + tokens], value[...], preferred_element_type=jnp.float32)
        total = part if total is None else total + part
        at += tokens
    out_ref[...] = total.astype(jnp.bfloat16)


def weight_kernel_held(count, place_ref, *refs):
    weight_kernel(count, place_ref, *refs[:-3], *refs[-2:])


def weight_rows(core, pieces, values, so_far, tile=512):
    rows, width = pieces[0].shape
    units = values[0].shape[1]
    total = rows * len(pieces)
    held = [] if so_far is None else [so_far]
    return pl.pallas_call(
        functools.partial(weight_kernel_held if held else weight_kernel, len(pieces)),
        grid_spec=pltpu.PrefetchScalarGridSpec(
            num_scalar_prefetch=1,
            grid=(units // tile,),
            in_specs=[pl.BlockSpec((rows, width), lambda j, _: (0, 0))] * len(pieces)
            + [pl.BlockSpec((value.shape[0], tile), lambda j, _: (0, j)) for value in values]
            + [ANY] * len(held),
            out_specs=pl.BlockSpec((width, tile), lambda j, core: (core[0], j)),
            scratch_shapes=[pltpu.VMEM((width, total), jnp.bfloat16)],
        ),
        out_shape=jax.ShapeDtypeStruct((2 * width, units), jnp.bfloat16),
        input_output_aliases={1 + len(pieces) + len(values): 0} if held else {},
        compiler_params=params(),
        cost_estimate=cost(2 * width * total * units, 2 * width * total + 2 * total * units + 2 * width * units),
    )(core, *pieces, *values, *held)


def after(values, *others):
    return lax.optimization_barrier((values, *others))[0]


def swap(values, axis, bits):
    size = lax.axis_size(axis)
    return lax.ppermute(values, axis, [(t, t ^ bits) for t in range(size)])


def exchange(values, axis):
    return lax.all_to_all(values, axis, split_axis=0, concat_axis=0, tiled=True)


def per_device(grad_out, down_weight, quantized, clip_mask, first_rot, second_rot, block_order):
    devices, groups = lax.axis_size("tensor"), lax.axis_size("dp")
    me, group = lax.axis_index("tensor"), lax.axis_index("dp")
    place = jnp.stack([me, group]).astype(jnp.int32)
    core = (me % 2).astype(jnp.int32)[None]
    block = first_rot.shape[1]
    units = quantized.shape[1]
    tokens = grad_out.shape[0]
    rows = tokens // CHUNKS
    top, low = quantized[: tokens // 2], quantized[tokens // 2 :]
    weights = down_weight, clip_mask, second_rot

    full0 = lax.all_gather(grad_out[:rows], "tensor", axis=0)
    x_top, y_top = swap(top, "dp", 1), swap(top, "dp", 2)
    full1 = lax.all_gather(grad_out[rows:], "tensor", axis=0)
    low_now = after(low, x_top, y_top)
    x_low, y_low = swap(low_now, "dp", 1), swap(low_now, "dp", 2)
    permuted, shards = project(place, [after(full0, x_top, y_top)], *weights, 0, groups)
    sent = exchange(permuted.reshape(devices, rows // devices, units), "tensor")
    first = [shard if m == 0 else swap(shard, "dp", m) for m, shard in enumerate(shards)]
    xy_top, xy_low = swap(x_top, "dp", 2), swap(y_low, "dp", 1)
    permuted, shards = project(place, [after(full1, permuted, x_low, y_low)], *weights, 1, groups)
    permuted = after(permuted, xy_top, xy_low)
    placed = reorder(block_order, after(sent, permuted, *first), block)
    sent = exchange(permuted.reshape(devices, rows // devices, units), "tensor")
    second = [shard if m == 0 else swap(after(shard, permuted, *first), "dp", m) for m, shard in enumerate(shards)]
    mine = [piece for pair in zip(first, second) for piece in pair]
    returned = exchange(after(placed, sent), "tensor").reshape(rows, units)
    placed = reorder(block_order, after(sent, placed, *mine), block)
    theirs = [swap(value, "tensor", 1) for value in mine]
    values = [quantized, x_top, x_low, y_top, y_low, xy_top, xy_low]
    grad_weight = weight_rows(core, mine, [quantized, *values[1:-1], after(xy_low, placed)], None)
    last = exchange(after(placed, returned, grad_weight), "tensor").reshape(rows, units)
    grad_weight = weight_rows(1 - core, theirs, values, grad_weight)
    grad_hidden = rotate(returned, first_rot, 0, CHUNKS, None)
    grad_hidden = rotate(last, first_rot, 1, CHUNKS, grad_hidden)
    return (grad_hidden, grad_weight)


def block_apply(values, rotations):
    count, width = rotations.shape[:2]
    shaped = values.reshape(values.shape[0], count, width)
    result = jnp.einsum("tbi,bji->tbj", shaped, rotations, preferred_element_type=jnp.float32)
    return result.reshape(values.shape[0], count * width).astype(jnp.bfloat16)


def per_device_wide(grad_out, down_weight, quantized, clip_mask, first_rot, second_rot, block_order):
    tokens, units = quantized.shape
    devices = lax.axis_size("tensor")
    gathered = lax.all_gather(quantized, "dp", axis=0, tiled=True)
    full = lax.all_gather(grad_out, "tensor", axis=1, tiled=True)
    rows = lax.all_to_all(full, "dp", split_axis=1, concat_axis=0, tiled=True)
    grad_weight = lax.dot_general(
        rows, gathered, (((0,), (0,)), ((), ())), preferred_element_type=jnp.float32
    ).astype(jnp.bfloat16)
    product = jnp.dot(full, down_weight, preferred_element_type=jnp.float32)
    permuted = block_apply((product * clip_mask).astype(jnp.bfloat16), second_rot)
    blocks, width = block_order.shape[0], first_rot.shape[1]
    inverse = jnp.zeros((blocks,), jnp.int32).at[block_order].set(jnp.arange(blocks, dtype=jnp.int32))
    received = lax.all_to_all(
        permuted.reshape(devices, tokens // devices, units), "tensor", split_axis=0, concat_axis=2, tiled=True
    )
    lead, items = received.shape[:2]
    placed = jnp.take(received.reshape(lead, items, blocks, width), inverse, axis=2)
    returned = lax.all_to_all(
        placed.reshape(lead, items, blocks * width), "tensor", split_axis=2, concat_axis=0, tiled=True
    )
    grad_hidden = block_apply(returned.reshape(tokens, units), first_rot)
    return (grad_hidden, grad_weight)


def solution(mesh):
    placed = (
        P("dp", "tensor"),
        P(None, "tensor"),
        P("dp", "tensor"),
        P("dp", "tensor"),
        P("tensor", None, None),
        P("tensor", None, None),
        P(),
    )
    short = mesh.shape["tensor"] == 8 and mesh.shape["dp"] == 4
    return jax.shard_map(
        per_device if short else per_device_wide,
        mesh=mesh,
        in_specs=placed,
        out_specs=(P("dp", "tensor"), P("dp", "tensor")),
        check_vma=False,
    )
```

```python
import functools

import jax
import jax.numpy as jnp
from jax import lax
from jax.experimental import pallas as pl
from jax.experimental.pallas import tpu as pltpu
from jax.sharding import PartitionSpec as P

CHUNKS = 2
VMEM_LIMIT = 56 * 1024 * 1024
ANY = pl.BlockSpec(memory_space=pl.ANY)


def rows_at(index, count):
    return pl.ds(pl.multiple_of(index * count, count), count)


def params(limit=VMEM_LIMIT):
    return pltpu.CompilerParams(vmem_limit_bytes=limit)


def cost(flops, nbytes):
    return pl.CostEstimate(flops=int(flops), bytes_accessed=int(nbytes), transcendentals=0)


def project_kernel(devices, groups, tile, chunk, place_ref, *refs):
    bufs, (w_ref, mask_ref, rot_ref, out_ref) = refs[:devices], refs[devices : devices + 4]
    shards, (dy, sems, shard_sems) = refs[devices + 4 : -3], refs[-3:]
    me, group = place_ref[0], place_ref[1]
    rows, width = dy.shape[0], dy.shape[1] // devices

    def gather(action):
        for x in range(devices):
            source = bufs[x]
            if source.shape[0] != rows:
                source = source.at[chunk * rows : (chunk + 1) * rows]
            action(pltpu.make_async_copy(source, dy.at[:, rows_at(me ^ x, width)], sems.at[x]))

    def share(action):
        for m, shard in enumerate(shards):
            source = dy.at[:, rows_at(2 * (group ^ m) + me % 2, width)]
            action(pltpu.make_async_copy(source, shard, shard_sems.at[m]))

    @pl.when(pl.program_id(0) == 0)
    def _():
        gather(lambda copy: copy.start())
        gather(lambda copy: copy.wait())
        share(lambda copy: copy.start())

    product = jnp.dot(dy[...], w_ref[...], preferred_element_type=jnp.float32)
    masked = (product * mask_ref[...].astype(jnp.float32)).astype(jnp.bfloat16)
    block = rot_ref.shape[1]
    for b in range(tile // block):
        turned = lax.dot_general(
            masked[:, b * block : (b + 1) * block],
            rot_ref[b],
            (((1,), (1,)), ((), ())),
            preferred_element_type=jnp.float32,
        )
        out_ref[:, b * block : (b + 1) * block] = turned.astype(jnp.bfloat16)

    @pl.when(pl.program_id(0) == pl.num_programs(0) - 1)
    def _():
        share(lambda copy: copy.wait())


def project(place, bufs, weight, mask, rot, chunk, groups, tile_blocks=4):
    devices = len(bufs)
    rows, width = bufs[-1].shape
    depth, units = weight.shape
    block = rot.shape[1]
    tile = tile_blocks * block
    permuted, *shards = pl.pallas_call(
        functools.partial(project_kernel, devices, groups, tile, chunk),
        grid_spec=pltpu.PrefetchScalarGridSpec(
            num_scalar_prefetch=1,
            grid=(units // tile,),
            in_specs=[ANY] * len(bufs)
            + [
                pl.BlockSpec((depth, tile), lambda j, _: (0, j)),
                pl.BlockSpec((rows, tile), lambda j, _: (chunk, j)),
                pl.BlockSpec((tile // block, block, block), lambda j, _: (j, 0, 0)),
            ],
            out_specs=[pl.BlockSpec((rows, tile), lambda j, _: (0, j))] + [ANY] * groups,
            scratch_shapes=[
                pltpu.VMEM((rows, depth), jnp.bfloat16),
                pltpu.SemaphoreType.DMA((devices,)),
                pltpu.SemaphoreType.DMA((groups,)),
            ],
        ),
        out_shape=[jax.ShapeDtypeStruct((rows, units), jnp.bfloat16)]
        + [jax.ShapeDtypeStruct((rows, width), jnp.bfloat16)] * groups,
        compiler_params=params(),
        cost_estimate=cost(2 * rows * depth * units, 2 * depth * units + 2 * rows * depth + 8 * rows * units),
    )(place, *bufs, weight, mask, rot)
    return permuted, shards


def reorder_kernel(block, order_ref, in_ref, out_ref):
    per = in_ref.shape[2] // block
    for source in range(in_ref.shape[0]):
        for b in range(per):
            to = order_ref[source * per + b]
            out_ref[to // per, :, rows_at(to % per, block)] = in_ref[source, :, b * block : (b + 1) * block]


def reorder(order, pieces, block):
    devices, rows, units = pieces.shape
    step = min(rows, 16)
    spec = pl.BlockSpec((devices, step, units), lambda i, _: (0, i, 0))
    return pl.pallas_call(
        functools.partial(reorder_kernel, block),
        grid_spec=pltpu.PrefetchScalarGridSpec(
            num_scalar_prefetch=1, grid=(rows // step,), in_specs=[spec], out_specs=spec
        ),
        out_shape=jax.ShapeDtypeStruct(pieces.shape, jnp.bfloat16),
        compiler_params=params(),
        cost_estimate=cost(0, 4 * devices * rows * units),
    )(order, pieces)


def rotate_kernel(piece_ref, rot_ref, *refs):
    out_ref = refs[-1]
    block = rot_ref.shape[1]
    for b in range(rot_ref.shape[0]):
        turned = lax.dot_general(
            piece_ref[:, b * block : (b + 1) * block],
            rot_ref[b],
            (((1,), (1,)), ((), ())),
            preferred_element_type=jnp.float32,
        )
        out_ref[:, b * block : (b + 1) * block] = turned.astype(jnp.bfloat16)


def rotate(piece, rot, chunk, chunks, so_far):
    rows, units = piece.shape
    block = rot.shape[1]
    tile = 8 * block
    held = [] if so_far is None else [so_far]
    return pl.pallas_call(
        rotate_kernel,
        grid=(units // tile,),
        in_specs=[
            pl.BlockSpec((rows, tile), lambda j: (0, j)),
            pl.BlockSpec((tile // block, block, block), lambda j: (j, 0, 0)),
        ]
        + [ANY] * len(held),
        out_specs=pl.BlockSpec((rows, tile), lambda j: (chunk, j)),
        out_shape=jax.ShapeDtypeStruct((rows * chunks, units), jnp.bfloat16),
        input_output_aliases={2: 0} if held else {},
        compiler_params=params(),
        cost_estimate=cost(2 * rows * units * block, 4 * rows * units),
    )(piece, rot, *held)


def weight_kernel(add, place_ref, *refs):
    groups = len(refs) - 4
    pieces, (q_ref, held_ref, out_ref, turned) = refs[:groups], refs[groups:]
    rows = pieces[0].shape[0]

    @pl.when(pl.program_id(0) == 0)
    def _():
        for m, piece in enumerate(pieces):
            turned[:, rows_at(place_ref[1] ^ m, rows)] = piece[...].T

    values = q_ref[...].reshape(groups * rows, q_ref.shape[-1])
    total = jnp.dot(turned[...], values, preferred_element_type=jnp.float32)
    if add:
        total = total + held_ref[...].astype(jnp.float32)
    out_ref[...] = total.astype(jnp.bfloat16)


def weight_kernel_first(place_ref, *refs):
    weight_kernel(False, place_ref, *refs[:-2], None, *refs[-2:])


def weight_rows(core, group, pieces, gathered, chunk, held, tile=512):
    rows, width = pieces[0].shape
    groups, _, _, units = gathered.shape
    total = groups * rows
    add = chunk > 0
    out_spec = pl.BlockSpec((width, tile), lambda j, place: (place[0], j))
    if held is None:
        kernel, extra = weight_kernel_first, []
    else:
        kernel, extra = functools.partial(weight_kernel, add), [out_spec if add else ANY]
    return pl.pallas_call(
        kernel,
        grid_spec=pltpu.PrefetchScalarGridSpec(
            num_scalar_prefetch=1,
            grid=(units // tile,),
            in_specs=[pl.BlockSpec((rows, width), lambda j, _: (0, 0))] * groups
            + [pl.BlockSpec((groups, None, rows, tile), lambda j, _: (0, chunk, 0, j))]
            + extra,
            out_specs=out_spec,
            scratch_shapes=[pltpu.VMEM((width, total), jnp.bfloat16)],
        ),
        out_shape=jax.ShapeDtypeStruct((2 * width, units), jnp.bfloat16),
        input_output_aliases={2 + groups: 0} if extra else {},
        compiler_params=params(),
        cost_estimate=cost(2 * width * total * units, 2 * width * total + 2 * total * units + 4 * width * units),
    )(jnp.stack([core, group]).astype(jnp.int32), *pieces, gathered, *([] if held is None else [held]))


def after(values, *others):
    return lax.optimization_barrier((values, *others))[0]


def swap(values, axis, bits):
    size = lax.axis_size(axis)
    return lax.ppermute(values, axis, [(t, t ^ bits) for t in range(size)])


def exchange(values, axis):
    return lax.all_to_all(values, axis, split_axis=0, concat_axis=0, tiled=True)


def token_exchange(pieces):
    return [piece if m == 0 else swap(piece, "dp", m) for m, piece in enumerate(pieces)]


def per_device(grad_out, down_weight, quantized, clip_mask, first_rot, second_rot, block_order):
    devices, groups = lax.axis_size("tensor"), lax.axis_size("dp")
    me, group = lax.axis_index("tensor"), lax.axis_index("dp")
    place = jnp.stack([me, group]).astype(jnp.int32)
    core = me % 2
    block = first_rot.shape[1]
    units = quantized.shape[1]
    rows = grad_out.shape[0] // CHUNKS
    weights = down_weight, clip_mask, second_rot
    gathered = lax.all_gather(quantized.reshape(CHUNKS, rows, units), "dp", axis=0)

    own = grad_out[:rows], grad_out[rows:]
    whole = swap(grad_out, "tensor", 1)
    far0, near0 = swap(own[0], "tensor", 4), swap(own[0], "tensor", 2)
    corner0 = swap(after(far0, near0), "tensor", 2)
    far1 = swap(after(own[1], far0, near0), "tensor", 4)
    corner1, near1 = swap(far1, "tensor", 2), swap(after(own[1], far1, corner0), "tensor", 2)

    def with_cores(near, far, corner):
        return [grad_out, whole] + [buf for values in (near, far, corner) for buf in (values, swap(values, "tensor", 1))]

    bufs = with_cores(near0, far0, corner0)
    bufs[-1] = after(bufs[-1], far1)
    permuted, shards = project(place, bufs, *weights, 0, groups)
    permuted = after(permuted, near1, corner1)
    sent = exchange(permuted.reshape(devices, rows // devices, units), "tensor")
    first = token_exchange(shards)
    bufs = with_cores(near1, far1, corner1)
    bufs[-1] = after(bufs[-1], permuted)
    permuted, shards = project(place, bufs, *weights, 1, groups)
    second = token_exchange(after(shard, *first) for shard in shards)
    placed = reorder(block_order, after(sent, permuted, *first), block)
    sent = exchange(permuted.reshape(devices, rows // devices, units), "tensor")
    returned = exchange(after(placed, sent), "tensor").reshape(rows, units)
    placed = reorder(block_order, after(sent, placed), block)
    other = [swap(value, "tensor", 1) for value in first]
    grad_weight = weight_rows(core, group, [after(first[0], placed), *first[1:]], gathered, 0, None)
    grad_weight = weight_rows(1 - core, group, other, gathered, 0, grad_weight)
    last = exchange(after(placed, returned, grad_weight, *second), "tensor").reshape(rows, units)
    other = [swap(value, "tensor", 1) for value in second]
    grad_weight = weight_rows(core, group, [after(second[0], returned), *second[1:]], gathered, 1, grad_weight)
    grad_weight = weight_rows(1 - core, group, other, gathered, 1, grad_weight)
    grad_hidden = rotate(returned, first_rot, 0, CHUNKS, None)
    grad_hidden = rotate(last, first_rot, 1, CHUNKS, grad_hidden)
    return (grad_hidden, grad_weight)


def block_apply(values, rotations):
    count, width = rotations.shape[:2]
    shaped = values.reshape(values.shape[0], count, width)
    result = jnp.einsum("tbi,bji->tbj", shaped, rotations, preferred_element_type=jnp.float32)
    return result.reshape(values.shape[0], count * width).astype(jnp.bfloat16)


def per_device_wide(grad_out, down_weight, quantized, clip_mask, first_rot, second_rot, block_order):
    tokens, units = quantized.shape
    devices = lax.axis_size("tensor")
    gathered = lax.all_gather(quantized, "dp", axis=0, tiled=True)
    full = lax.all_gather(grad_out, "tensor", axis=1, tiled=True)
    rows = lax.all_to_all(full, "dp", split_axis=1, concat_axis=0, tiled=True)
    grad_weight = lax.dot_general(
        rows, gathered, (((0,), (0,)), ((), ())), preferred_element_type=jnp.float32
    ).astype(jnp.bfloat16)
    product = jnp.dot(full, down_weight, preferred_element_type=jnp.float32)
    permuted = block_apply((product * clip_mask).astype(jnp.bfloat16), second_rot)
    blocks, width = block_order.shape[0], first_rot.shape[1]
    inverse = jnp.zeros((blocks,), jnp.int32).at[block_order].set(jnp.arange(blocks, dtype=jnp.int32))
    received = lax.all_to_all(
        permuted.reshape(devices, tokens // devices, units), "tensor", split_axis=0, concat_axis=2, tiled=True
    )
    lead, items = received.shape[:2]
    placed = jnp.take(received.reshape(lead, items, blocks, width), inverse, axis=2)
    returned = lax.all_to_all(
        placed.reshape(lead, items, blocks * width), "tensor", split_axis=2, concat_axis=0, tiled=True
    )
    grad_hidden = block_apply(returned.reshape(tokens, units), first_rot)
    return (grad_hidden, grad_weight)


def solution(mesh):
    placed = (
        P("dp", "tensor"),
        P(None, "tensor"),
        P("dp", "tensor"),
        P("dp", "tensor"),
        P("tensor", None, None),
        P("tensor", None, None),
        P(),
    )
    short = mesh.shape["tensor"] == 8 and mesh.shape["dp"] == 4
    return jax.shard_map(
        per_device if short else per_device_wide,
        mesh=mesh,
        in_specs=placed,
        out_specs=(P("dp", "tensor"), P("dp", "tensor")),
        check_vma=False,
    )
```

```python
import functools

import jax
import jax.numpy as jnp
from jax import lax
from jax.experimental import pallas as pl
from jax.experimental.pallas import tpu as pltpu
from jax.sharding import PartitionSpec as P

CHUNKS = 2
VMEM_LIMIT = 56 * 1024 * 1024
ANY = pl.BlockSpec(memory_space=pl.ANY)


def rows_at(index, count):
    return pl.ds(pl.multiple_of(index * count, count), count)


def params(limit=VMEM_LIMIT):
    return pltpu.CompilerParams(vmem_limit_bytes=limit)


def cost(flops, nbytes):
    return pl.CostEstimate(flops=int(flops), bytes_accessed=int(nbytes), transcendentals=0)


def project_kernel(devices, groups, tile, chunk, place_ref, *refs):
    bufs, (w_ref, mask_ref, rot_ref, out_ref) = refs[:devices], refs[devices : devices + 4]
    shards, (dy, sems, shard_sems) = refs[devices + 4 : -3], refs[-3:]
    me, group = place_ref[0], place_ref[1]
    rows, width = dy.shape[0], dy.shape[1] // devices

    def gather(action):
        for x in range(devices):
            source = bufs[x]
            if source.shape[0] != rows:
                source = source.at[chunk * rows : (chunk + 1) * rows]
            action(pltpu.make_async_copy(source, dy.at[:, rows_at(me ^ x, width)], sems.at[x]))

    def share(action):
        for m, shard in enumerate(shards):
            source = dy.at[:, rows_at(2 * (group ^ m) + me % 2, width)]
            action(pltpu.make_async_copy(source, shard, shard_sems.at[m]))

    @pl.when(pl.program_id(0) == 0)
    def _():
        gather(lambda copy: copy.start())
        gather(lambda copy: copy.wait())
        share(lambda copy: copy.start())

    product = jnp.dot(dy[...], w_ref[...], preferred_element_type=jnp.float32)
    masked = (product * mask_ref[...].astype(jnp.float32)).astype(jnp.bfloat16)
    block = rot_ref.shape[1]
    for b in range(tile // block):
        turned = lax.dot_general(
            masked[:, b * block : (b + 1) * block],
            rot_ref[b],
            (((1,), (1,)), ((), ())),
            preferred_element_type=jnp.float32,
        )
        out_ref[:, b * block : (b + 1) * block] = turned.astype(jnp.bfloat16)

    @pl.when(pl.program_id(0) == pl.num_programs(0) - 1)
    def _():
        share(lambda copy: copy.wait())


def project(place, bufs, weight, mask, rot, chunk, groups, tile_blocks=4):
    devices = len(bufs)
    rows, width = bufs[-1].shape
    depth, units = weight.shape
    block = rot.shape[1]
    tile = tile_blocks * block
    permuted, *shards = pl.pallas_call(
        functools.partial(project_kernel, devices, groups, tile, chunk),
        grid_spec=pltpu.PrefetchScalarGridSpec(
            num_scalar_prefetch=1,
            grid=(units // tile,),
            in_specs=[ANY] * len(bufs)
            + [
                pl.BlockSpec((depth, tile), lambda j, _: (0, j)),
                pl.BlockSpec((rows, tile), lambda j, _: (chunk, j)),
                pl.BlockSpec((tile // block, block, block), lambda j, _: (j, 0, 0)),
            ],
            out_specs=[pl.BlockSpec((rows, tile), lambda j, _: (0, j))] + [ANY] * groups,
            scratch_shapes=[
                pltpu.VMEM((rows, depth), jnp.bfloat16),
                pltpu.SemaphoreType.DMA((devices,)),
                pltpu.SemaphoreType.DMA((groups,)),
            ],
        ),
        out_shape=[jax.ShapeDtypeStruct((rows, units), jnp.bfloat16)]
        + [jax.ShapeDtypeStruct((rows, width), jnp.bfloat16)] * groups,
        compiler_params=params(),
        cost_estimate=cost(2 * rows * depth * units, 2 * depth * units + 2 * rows * depth + 8 * rows * units),
    )(place, *bufs, weight, mask, rot)
    return permuted, shards


def reorder_kernel(block, order_ref, in_ref, out_ref):
    per = in_ref.shape[2] // block
    for source in range(in_ref.shape[0]):
        for b in range(per):
            to = order_ref[source * per + b]
            out_ref[to // per, :, rows_at(to % per, block)] = in_ref[source, :, b * block : (b + 1) * block]


def reorder(order, pieces, block):
    devices, rows, units = pieces.shape
    step = min(rows, 16)
    spec = pl.BlockSpec((devices, step, units), lambda i, _: (0, i, 0))
    return pl.pallas_call(
        functools.partial(reorder_kernel, block),
        grid_spec=pltpu.PrefetchScalarGridSpec(
            num_scalar_prefetch=1, grid=(rows // step,), in_specs=[spec], out_specs=spec
        ),
        out_shape=jax.ShapeDtypeStruct(pieces.shape, jnp.bfloat16),
        compiler_params=params(),
        cost_estimate=cost(0, 4 * devices * rows * units),
    )(order, pieces)


def rotate_kernel(piece_ref, rot_ref, *refs):
    out_ref = refs[-1]
    block = rot_ref.shape[1]
    for b in range(rot_ref.shape[0]):
        turned = lax.dot_general(
            piece_ref[:, b * block : (b + 1) * block],
            rot_ref[b],
            (((1,), (1,)), ((), ())),
            preferred_element_type=jnp.float32,
        )
        out_ref[:, b * block : (b + 1) * block] = turned.astype(jnp.bfloat16)


def rotate(piece, rot, chunk, chunks, so_far):
    rows, units = piece.shape
    block = rot.shape[1]
    tile = 8 * block
    held = [] if so_far is None else [so_far]
    return pl.pallas_call(
        rotate_kernel,
        grid=(units // tile,),
        in_specs=[
            pl.BlockSpec((rows, tile), lambda j: (0, j)),
            pl.BlockSpec((tile // block, block, block), lambda j: (j, 0, 0)),
        ]
        + [ANY] * len(held),
        out_specs=pl.BlockSpec((rows, tile), lambda j: (chunk, j)),
        out_shape=jax.ShapeDtypeStruct((rows * chunks, units), jnp.bfloat16),
        input_output_aliases={2: 0} if held else {},
        compiler_params=params(),
        cost_estimate=cost(2 * rows * units * block, 4 * rows * units),
    )(piece, rot, *held)


def weight_kernel(add, place_ref, *refs):
    groups = len(refs) - 4
    pieces, (q_ref, held_ref, out_ref, turned) = refs[:groups], refs[groups:]
    rows = pieces[0].shape[0]

    @pl.when(pl.program_id(0) == 0)
    def _():
        for m, piece in enumerate(pieces):
            turned[:, rows_at(place_ref[1] ^ m, rows)] = piece[...].T

    values = q_ref[...].reshape(groups * rows, q_ref.shape[-1])
    total = jnp.dot(turned[...], values, preferred_element_type=jnp.float32)
    if add:
        total = total + held_ref[...].astype(jnp.float32)
    out_ref[...] = total.astype(jnp.bfloat16)


def weight_kernel_first(place_ref, *refs):
    weight_kernel(False, place_ref, *refs[:-2], None, *refs[-2:])


def weight_rows(core, group, pieces, gathered, chunk, held, tile=512):
    rows, width = pieces[0].shape
    groups, _, _, units = gathered.shape
    total = groups * rows
    add = chunk > 0
    out_spec = pl.BlockSpec((width, tile), lambda j, place: (place[0], j))
    if held is None:
        kernel, extra = weight_kernel_first, []
    else:
        kernel, extra = functools.partial(weight_kernel, add), [out_spec if add else ANY]
    return pl.pallas_call(
        kernel,
        grid_spec=pltpu.PrefetchScalarGridSpec(
            num_scalar_prefetch=1,
            grid=(units // tile,),
            in_specs=[pl.BlockSpec((rows, width), lambda j, _: (0, 0))] * groups
            + [pl.BlockSpec((groups, None, rows, tile), lambda j, _: (0, chunk, 0, j))]
            + extra,
            out_specs=out_spec,
            scratch_shapes=[pltpu.VMEM((width, total), jnp.bfloat16)],
        ),
        out_shape=jax.ShapeDtypeStruct((2 * width, units), jnp.bfloat16),
        input_output_aliases={2 + groups: 0} if extra else {},
        compiler_params=params(),
        cost_estimate=cost(2 * width * total * units, 2 * width * total + 2 * total * units + 4 * width * units),
    )(jnp.stack([core, group]).astype(jnp.int32), *pieces, gathered, *([] if held is None else [held]))


def after(values, *others):
    return lax.optimization_barrier((values, *others))[0]


def swap(values, axis, bits):
    size = lax.axis_size(axis)
    return lax.ppermute(values, axis, [(t, t ^ bits) for t in range(size)])


def exchange(values, axis):
    return lax.all_to_all(values, axis, split_axis=0, concat_axis=0, tiled=True)


def token_exchange(pieces):
    return [piece if m == 0 else swap(piece, "dp", m) for m, piece in enumerate(pieces)]


def per_device(grad_out, down_weight, quantized, clip_mask, first_rot, second_rot, block_order):
    devices, groups = lax.axis_size("tensor"), lax.axis_size("dp")
    me, group = lax.axis_index("tensor"), lax.axis_index("dp")
    place = jnp.stack([me, group]).astype(jnp.int32)
    core = me % 2
    block = first_rot.shape[1]
    units = quantized.shape[1]
    rows = grad_out.shape[0] // CHUNKS
    weights = down_weight, clip_mask, second_rot
    gathered = lax.all_gather(quantized.reshape(CHUNKS, rows, units), "dp", axis=0)

    own = grad_out[:rows], grad_out[rows:]
    whole = swap(grad_out, "tensor", 1)
    far0, near0 = swap(own[0], "tensor", 4), swap(own[0], "tensor", 2)
    corner0 = swap(after(far0, near0), "tensor", 2)
    far1 = swap(after(own[1], corner0), "tensor", 4)
    corner1, near1 = swap(far1, "tensor", 2), swap(after(own[1], corner0), "tensor", 2)

    def with_cores(near, far, corner):
        return [grad_out, whole] + [buf for values in (near, far, corner) for buf in (values, swap(values, "tensor", 1))]

    bufs = with_cores(near0, far0, corner0)
    permuted, shards = project(place, bufs, *weights, 0, groups)
    permuted = after(permuted, near1, far1)
    sent = exchange(permuted.reshape(devices, rows // devices, units), "tensor")
    first = token_exchange(shards)
    bufs = with_cores(near1, far1, corner1)
    bufs[-1] = after(bufs[-1], permuted)
    permuted, shards = project(place, bufs, *weights, 1, groups)
    second = token_exchange(after(shard, *first) for shard in shards)
    placed = reorder(block_order, after(sent, permuted, *first), block)
    sent = exchange(permuted.reshape(devices, rows // devices, units), "tensor")
    returned = exchange(after(placed, sent), "tensor").reshape(rows, units)
    placed = reorder(block_order, after(sent, placed), block)
    other = [swap(value, "tensor", 1) for value in first]
    grad_weight = weight_rows(core, group, [after(first[0], placed), *first[1:]], gathered, 0, None)
    grad_weight = weight_rows(1 - core, group, other, gathered, 0, grad_weight)
    last = exchange(after(placed, returned, grad_weight, *second), "tensor").reshape(rows, units)
    other = [swap(value, "tensor", 1) for value in second]
    grad_weight = weight_rows(core, group, [after(second[0], returned), *second[1:]], gathered, 1, grad_weight)
    grad_weight = weight_rows(1 - core, group, other, gathered, 1, grad_weight)
    grad_hidden = rotate(returned, first_rot, 0, CHUNKS, None)
    grad_hidden = rotate(last, first_rot, 1, CHUNKS, grad_hidden)
    return (grad_hidden, grad_weight)


def block_apply(values, rotations):
    count, width = rotations.shape[:2]
    shaped = values.reshape(values.shape[0], count, width)
    result = jnp.einsum("tbi,bji->tbj", shaped, rotations, preferred_element_type=jnp.float32)
    return result.reshape(values.shape[0], count * width).astype(jnp.bfloat16)


def per_device_wide(grad_out, down_weight, quantized, clip_mask, first_rot, second_rot, block_order):
    tokens, units = quantized.shape
    devices = lax.axis_size("tensor")
    gathered = lax.all_gather(quantized, "dp", axis=0, tiled=True)
    full = lax.all_gather(grad_out, "tensor", axis=1, tiled=True)
    rows = lax.all_to_all(full, "dp", split_axis=1, concat_axis=0, tiled=True)
    grad_weight = lax.dot_general(
        rows, gathered, (((0,), (0,)), ((), ())), preferred_element_type=jnp.float32
    ).astype(jnp.bfloat16)
    product = jnp.dot(full, down_weight, preferred_element_type=jnp.float32)
    permuted = block_apply((product * clip_mask).astype(jnp.bfloat16), second_rot)
    blocks, width = block_order.shape[0], first_rot.shape[1]
    inverse = jnp.zeros((blocks,), jnp.int32).at[block_order].set(jnp.arange(blocks, dtype=jnp.int32))
    received = lax.all_to_all(
        permuted.reshape(devices, tokens // devices, units), "tensor", split_axis=0, concat_axis=2, tiled=True
    )
    lead, items = received.shape[:2]
    placed = jnp.take(received.reshape(lead, items, blocks, width), inverse, axis=2)
    returned = lax.all_to_all(
        placed.reshape(lead, items, blocks * width), "tensor", split_axis=2, concat_axis=0, tiled=True
    )
    grad_hidden = block_apply(returned.reshape(tokens, units), first_rot)
    return (grad_hidden, grad_weight)


def solution(mesh):
    placed = (
        P("dp", "tensor"),
        P(None, "tensor"),
        P("dp", "tensor"),
        P("dp", "tensor"),
        P("tensor", None, None),
        P("tensor", None, None),
        P(),
    )
    short = mesh.shape["tensor"] == 8 and mesh.shape["dp"] == 4
    return jax.shard_map(
        per_device if short else per_device_wide,
        mesh=mesh,
        in_specs=placed,
        out_specs=(P("dp", "tensor"), P("dp", "tensor")),
        check_vma=False,
    )
```

```python
import functools

import jax
import jax.numpy as jnp
from jax import lax
from jax.experimental import pallas as pl
from jax.experimental.pallas import tpu as pltpu
from jax.sharding import PartitionSpec as P

CHUNKS = 2
VMEM_LIMIT = 56 * 1024 * 1024
ANY = pl.BlockSpec(memory_space=pl.ANY)


def rows_at(index, count):
    return pl.ds(pl.multiple_of(index * count, count), count)


def params(limit=VMEM_LIMIT):
    return pltpu.CompilerParams(vmem_limit_bytes=limit)


def cost(flops, nbytes):
    return pl.CostEstimate(flops=int(flops), bytes_accessed=int(nbytes), transcendentals=0)


def project_kernel(devices, groups, tile, chunk, place_ref, *refs):
    bufs, (w_ref, mask_ref, rot_ref, out_ref) = refs[:devices], refs[devices : devices + 4]
    shards, (dy, sems, shard_sems) = refs[devices + 4 : -3], refs[-3:]
    me, group = place_ref[0], place_ref[1]
    rows, width = dy.shape[0], dy.shape[1] // devices

    def gather(action):
        for x in range(devices):
            source = bufs[x]
            if source.shape[0] != rows:
                source = source.at[chunk * rows : (chunk + 1) * rows]
            action(pltpu.make_async_copy(source, dy.at[:, rows_at(me ^ x, width)], sems.at[x]))

    def share(action):
        for m, shard in enumerate(shards):
            source = dy.at[:, rows_at(2 * (group ^ m) + me % 2, width)]
            action(pltpu.make_async_copy(source, shard, shard_sems.at[m]))

    @pl.when(pl.program_id(0) == 0)
    def _():
        gather(lambda copy: copy.start())
        gather(lambda copy: copy.wait())
        share(lambda copy: copy.start())

    product = jnp.dot(dy[...], w_ref[...], preferred_element_type=jnp.float32)
    masked = (product * mask_ref[...].astype(jnp.float32)).astype(jnp.bfloat16)
    block = rot_ref.shape[1]
    for b in range(tile // block):
        turned = lax.dot_general(
            masked[:, b * block : (b + 1) * block],
            rot_ref[b],
            (((1,), (1,)), ((), ())),
            preferred_element_type=jnp.float32,
        )
        out_ref[:, b * block : (b + 1) * block] = turned.astype(jnp.bfloat16)

    @pl.when(pl.program_id(0) == pl.num_programs(0) - 1)
    def _():
        share(lambda copy: copy.wait())


def project(place, bufs, weight, mask, rot, chunk, groups, tile_blocks=4):
    devices = len(bufs)
    rows, width = bufs[-1].shape
    depth, units = weight.shape
    block = rot.shape[1]
    tile = tile_blocks * block
    permuted, *shards = pl.pallas_call(
        functools.partial(project_kernel, devices, groups, tile, chunk),
        grid_spec=pltpu.PrefetchScalarGridSpec(
            num_scalar_prefetch=1,
            grid=(units // tile,),
            in_specs=[ANY] * len(bufs)
            + [
                pl.BlockSpec((depth, tile), lambda j, _: (0, j)),
                pl.BlockSpec((rows, tile), lambda j, _: (chunk, j)),
                pl.BlockSpec((tile // block, block, block), lambda j, _: (j, 0, 0)),
            ],
            out_specs=[pl.BlockSpec((rows, tile), lambda j, _: (0, j))] + [ANY] * groups,
            scratch_shapes=[
                pltpu.VMEM((rows, depth), jnp.bfloat16),
                pltpu.SemaphoreType.DMA((devices,)),
                pltpu.SemaphoreType.DMA((groups,)),
            ],
        ),
        out_shape=[jax.ShapeDtypeStruct((rows, units), jnp.bfloat16)]
        + [jax.ShapeDtypeStruct((rows, width), jnp.bfloat16)] * groups,
        compiler_params=params(),
        cost_estimate=cost(2 * rows * depth * units, 2 * depth * units + 2 * rows * depth + 8 * rows * units),
    )(place, *bufs, weight, mask, rot)
    return permuted, shards


def reorder_kernel(block, order_ref, in_ref, out_ref):
    per = in_ref.shape[2] // block
    for source in range(in_ref.shape[0]):
        for b in range(per):
            to = order_ref[source * per + b]
            out_ref[to // per, :, rows_at(to % per, block)] = in_ref[source, :, b * block : (b + 1) * block]


def reorder(order, pieces, block):
    devices, rows, units = pieces.shape
    step = min(rows, 16)
    spec = pl.BlockSpec((devices, step, units), lambda i, _: (0, i, 0))
    return pl.pallas_call(
        functools.partial(reorder_kernel, block),
        grid_spec=pltpu.PrefetchScalarGridSpec(
            num_scalar_prefetch=1, grid=(rows // step,), in_specs=[spec], out_specs=spec
        ),
        out_shape=jax.ShapeDtypeStruct(pieces.shape, jnp.bfloat16),
        compiler_params=params(),
        cost_estimate=cost(0, 4 * devices * rows * units),
    )(order, pieces)


def rotate_kernel(piece_ref, rot_ref, *refs):
    out_ref = refs[-1]
    block = rot_ref.shape[1]
    for b in range(rot_ref.shape[0]):
        turned = lax.dot_general(
            piece_ref[:, b * block : (b + 1) * block],
            rot_ref[b],
            (((1,), (1,)), ((), ())),
            preferred_element_type=jnp.float32,
        )
        out_ref[:, b * block : (b + 1) * block] = turned.astype(jnp.bfloat16)


def rotate(piece, rot, chunk, chunks, so_far):
    rows, units = piece.shape
    block = rot.shape[1]
    tile = 4 * block
    held = [] if so_far is None else [so_far]
    return pl.pallas_call(
        rotate_kernel,
        grid=(units // tile,),
        in_specs=[
            pl.BlockSpec((rows, tile), lambda j: (0, j)),
            pl.BlockSpec((tile // block, block, block), lambda j: (j, 0, 0)),
        ]
        + [ANY] * len(held),
        out_specs=pl.BlockSpec((rows, tile), lambda j: (chunk, j)),
        out_shape=jax.ShapeDtypeStruct((rows * chunks, units), jnp.bfloat16),
        input_output_aliases={2: 0} if held else {},
        compiler_params=params(),
        cost_estimate=cost(2 * rows * units * block, 4 * rows * units),
    )(piece, rot, *held)


def weight_kernel(add, place_ref, *refs):
    groups = len(refs) - 4
    pieces, (q_ref, held_ref, out_ref, turned) = refs[:groups], refs[groups:]
    rows = pieces[0].shape[0]

    @pl.when(pl.program_id(0) == 0)
    def _():
        for m, piece in enumerate(pieces):
            turned[:, rows_at(place_ref[1] ^ m, rows)] = piece[...].T

    values = q_ref[...].reshape(groups * rows, q_ref.shape[-1])
    total = jnp.dot(turned[...], values, preferred_element_type=jnp.float32)
    if add:
        total = total + held_ref[...].astype(jnp.float32)
    out_ref[...] = total.astype(jnp.bfloat16)


def weight_kernel_first(place_ref, *refs):
    weight_kernel(False, place_ref, *refs[:-2], None, *refs[-2:])


def weight_rows(core, group, pieces, gathered, chunk, held, tile=512):
    rows, width = pieces[0].shape
    groups, _, _, units = gathered.shape
    total = groups * rows
    add = chunk > 0
    out_spec = pl.BlockSpec((width, tile), lambda j, place: (place[0], j))
    if held is None:
        kernel, extra = weight_kernel_first, []
    else:
        kernel, extra = functools.partial(weight_kernel, add), [out_spec if add else ANY]
    return pl.pallas_call(
        kernel,
        grid_spec=pltpu.PrefetchScalarGridSpec(
            num_scalar_prefetch=1,
            grid=(units // tile,),
            in_specs=[pl.BlockSpec((rows, width), lambda j, _: (0, 0))] * groups
            + [pl.BlockSpec((groups, None, rows, tile), lambda j, _: (0, chunk, 0, j))]
            + extra,
            out_specs=out_spec,
            scratch_shapes=[pltpu.VMEM((width, total), jnp.bfloat16)],
        ),
        out_shape=jax.ShapeDtypeStruct((2 * width, units), jnp.bfloat16),
        input_output_aliases={2 + groups: 0} if extra else {},
        compiler_params=params(),
        cost_estimate=cost(2 * width * total * units, 2 * width * total + 2 * total * units + 4 * width * units),
    )(jnp.stack([core, group]).astype(jnp.int32), *pieces, gathered, *([] if held is None else [held]))


def after(values, *others):
    return lax.optimization_barrier((values, *others))[0]


def swap(values, axis, bits):
    size = lax.axis_size(axis)
    return lax.ppermute(values, axis, [(t, t ^ bits) for t in range(size)])


def exchange(values, axis):
    return lax.all_to_all(values, axis, split_axis=0, concat_axis=0, tiled=True)


def token_exchange(pieces):
    return [piece if m == 0 else swap(piece, "dp", m) for m, piece in enumerate(pieces)]


def per_device(grad_out, down_weight, quantized, clip_mask, first_rot, second_rot, block_order):
    devices, groups = lax.axis_size("tensor"), lax.axis_size("dp")
    me, group = lax.axis_index("tensor"), lax.axis_index("dp")
    place = jnp.stack([me, group]).astype(jnp.int32)
    core = me % 2
    block = first_rot.shape[1]
    units = quantized.shape[1]
    rows = grad_out.shape[0] // CHUNKS
    weights = down_weight, clip_mask, second_rot
    gathered = lax.all_gather(quantized.reshape(CHUNKS, rows, units), "dp", axis=0)

    own = grad_out[:rows], grad_out[rows:]
    whole = swap(grad_out, "tensor", 1)
    far0, near0 = swap(own[0], "tensor", 4), swap(own[0], "tensor", 2)
    corner0 = swap(after(far0, near0), "tensor", 2)
    far1 = swap(after(own[1], far0, near0), "tensor", 4)
    corner1, near1 = swap(far1, "tensor", 2), swap(after(own[1], far1, corner0), "tensor", 2)

    def with_cores(near, far, corner):
        return [grad_out, whole] + [buf for values in (near, far, corner) for buf in (values, swap(values, "tensor", 1))]

    bufs = with_cores(near0, far0, corner0)
    bufs[-1] = after(bufs[-1], far1)
    permuted, shards = project(place, bufs, *weights, 0, groups)
    permuted = after(permuted, near1, corner1)
    sent = exchange(permuted.reshape(devices, rows // devices, units), "tensor")
    first = token_exchange(shards)
    bufs = with_cores(near1, far1, corner1)
    bufs[-1] = after(bufs[-1], permuted)
    permuted, shards = project(place, bufs, *weights, 1, groups)
    second = token_exchange(after(shard, *first) for shard in shards)
    placed = reorder(block_order, after(sent, permuted, *first), block)
    sent = exchange(permuted.reshape(devices, rows // devices, units), "tensor")
    returned = exchange(after(placed, sent), "tensor").reshape(rows, units)
    placed = reorder(block_order, after(sent, placed), block)
    other = [swap(value, "tensor", 1) for value in first]
    grad_weight = weight_rows(core, group, [after(first[0], placed), *first[1:]], gathered, 0, None)
    grad_weight = weight_rows(1 - core, group, other, gathered, 0, grad_weight)
    last = exchange(after(placed, returned, grad_weight, *second), "tensor").reshape(rows, units)
    other = [swap(value, "tensor", 1) for value in second]
    grad_weight = weight_rows(core, group, [after(second[0], returned), *second[1:]], gathered, 1, grad_weight)
    grad_weight = weight_rows(1 - core, group, other, gathered, 1, grad_weight)
    grad_hidden = rotate(returned, first_rot, 0, CHUNKS, None)
    grad_hidden = rotate(last, first_rot, 1, CHUNKS, grad_hidden)
    return (grad_hidden, grad_weight)


def block_apply(values, rotations):
    count, width = rotations.shape[:2]
    shaped = values.reshape(values.shape[0], count, width)
    result = jnp.einsum("tbi,bji->tbj", shaped, rotations, preferred_element_type=jnp.float32)
    return result.reshape(values.shape[0], count * width).astype(jnp.bfloat16)


def per_device_wide(grad_out, down_weight, quantized, clip_mask, first_rot, second_rot, block_order):
    tokens, units = quantized.shape
    devices = lax.axis_size("tensor")
    gathered = lax.all_gather(quantized, "dp", axis=0, tiled=True)
    full = lax.all_gather(grad_out, "tensor", axis=1, tiled=True)
    rows = lax.all_to_all(full, "dp", split_axis=1, concat_axis=0, tiled=True)
    grad_weight = lax.dot_general(
        rows, gathered, (((0,), (0,)), ((), ())), preferred_element_type=jnp.float32
    ).astype(jnp.bfloat16)
    product = jnp.dot(full, down_weight, preferred_element_type=jnp.float32)
    permuted = block_apply((product * clip_mask).astype(jnp.bfloat16), second_rot)
    blocks, width = block_order.shape[0], first_rot.shape[1]
    inverse = jnp.zeros((blocks,), jnp.int32).at[block_order].set(jnp.arange(blocks, dtype=jnp.int32))
    received = lax.all_to_all(
        permuted.reshape(devices, tokens // devices, units), "tensor", split_axis=0, concat_axis=2, tiled=True
    )
    lead, items = received.shape[:2]
    placed = jnp.take(received.reshape(lead, items, blocks, width), inverse, axis=2)
    returned = lax.all_to_all(
        placed.reshape(lead, items, blocks * width), "tensor", split_axis=2, concat_axis=0, tiled=True
    )
    grad_hidden = block_apply(returned.reshape(tokens, units), first_rot)
    return (grad_hidden, grad_weight)


def solution(mesh):
    placed = (
        P("dp", "tensor"),
        P(None, "tensor"),
        P("dp", "tensor"),
        P("dp", "tensor"),
        P("tensor", None, None),
        P("tensor", None, None),
        P(),
    )
    short = mesh.shape["tensor"] == 8 and mesh.shape["dp"] == 4
    return jax.shard_map(
        per_device if short else per_device_wide,
        mesh=mesh,
        in_specs=placed,
        out_specs=(P("dp", "tensor"), P("dp", "tensor")),
        check_vma=False,
    )
```
